1024 devices in a mesh: pipe: 8 (over y), ctx: 32 (over z, core), tp: 4 (over x).
Axes of the slice: x: 4, y: 8, z: 16, core: 2. Of those that a mesh axis runs over, the one named last changes fastest.
Arguments:
- queries: bfloat16 [8, 4096, 32, 128], P('pipe', 'ctx', 'tp'), may hold values from -45 to 45
- key_value: bfloat16 [8, 2, 4096, 8, 128], P('pipe', None, 'ctx', 'tp'), may hold values from -6 to 6
- mamba_in: bfloat16 [8, 4096, 8192], P('pipe', 'ctx', 'tp'), may hold values from -6 to 6
- gate_in: bfloat16 [8, 4096, 8192], P('pipe', 'ctx', 'tp'), may hold values from -6 to 6
- step_low: bfloat16 [8, 4096, 512], P('pipe', 'ctx'), may hold values from -3 to 3
- step_weight: bfloat16 [8, 512, 8192], P('pipe', None, 'tp'), may hold values from -0.25 to 0.25
- step_bias: float32 [8, 8192], P('pipe', 'tp'), may hold values from -4.6 to -3.2
- decay_rate: float32 [8, 8, 8192], P('pipe', None, 'tp'), may hold values from 0.0061035156 to 2.5
- conv_weight: float32 [8, 4, 8192], P('pipe', None, 'tp'), may hold values from -3 to 3
- conv_bias: float32 [8, 8192], P('pipe', 'tp'), may hold values from -3 to 3
- state_weight: bfloat16 [8, 8192, 16], P('pipe', 'tp'), may hold values from -0.0625 to 0.0625
- skip_gain: float32 [8, 8192], P('pipe', 'tp'), may hold values from 0.5 to 1.5
Outputs:
- attended: bfloat16 [8, 4096, 32, 128], P('pipe', 'ctx', 'tp')
- mamba_out: bfloat16 [8, 4096, 8192], P('pipe', 'ctx', 'tp')
The draws below stay inside these ranges and needn't reach their ends.
All inputs are finite; a program needn't handle non-finite values.
Results may differ from the reference program's by a relative error of at most 0.023.
Values may be sent and summed in bfloat16 or wider, within the bound.
No kernel may reach another device: no remote copies, remote signals or barrier semaphores. Data moves between devices by JAX's collectives and lax.ppermute only.
A program may use at most 64 MiB of HBM per device.

```python
import math
import jax
import jax.numpy as jnp
from jax import lax

Q_HEADS = 32
KV_HEADS = 8
HEAD_DIM = 128
INNER = 8192
STATE = 8
STEP_RANK = 512
CONV = 4
SEQ = 4096
SECTIONS = 8


def attention_inputs(key):
    key_part = jax.random.fold_in(key, 11)
    value_part = jax.random.fold_in(key, 12)
    query_part = jax.random.fold_in(key, 13)
    key_shape = (SECTIONS, SEQ, KV_HEADS, HEAD_DIM)
    query_shape = (SECTIONS, SEQ, Q_HEADS, HEAD_DIM)
    keys = jax.random.truncated_normal(key_part, -6.0, 6.0, key_shape, jnp.float32)
    values = jax.random.truncated_normal(value_part, -6.0, 6.0, key_shape, jnp.float32)
    queries = jax.random.truncated_normal(query_part, -6.0, 6.0, query_shape, jnp.float32)
    return (queries, jnp.stack([keys, values], axis=1))


def draw_queries(key, part):
    return attention_inputs(key)[0].astype(jnp.bfloat16)


def draw_key_value(key, part):
    return attention_inputs(key)[1].astype(jnp.bfloat16)


def draw_decay_rate(key, part):
    kind_key = jax.random.fold_in(key, 21)
    fast_key = jax.random.fold_in(key, 22)
    slow_key = jax.random.fold_in(key, 23)
    shape = (SECTIONS, STATE, INNER)
    fast_channel = jax.random.bernoulli(kind_key, 0.5, (SECTIONS, 1, INNER))
    slow_rate = jnp.exp(jax.random.uniform(slow_key, shape, jnp.float32, math.log(0.5), math.log(2.0))) / (0.02 * SEQ)
    fast_rate = jnp.exp(jax.random.uniform(fast_key, shape, jnp.float32, math.log(0.8), math.log(2.5)))
    return jnp.where(fast_channel, fast_rate, slow_rate)


def levels(stream_key, shape, pieces, low, top_value):
    gain = 1.0
    for axis_at, shards_of in pieces:
        heights = jax.random.uniform(jax.random.fold_in(jax.random.fold_in(stream_key, 6), axis_at), (shards_of,), jnp.float32, low / len(pieces), top_value / len(pieces))
        gain = gain * jnp.repeat(jnp.exp(heights), shape[axis_at] // shards_of).reshape((-1,) + (1,) * (len(shape) - 1 - axis_at))
    return gain


def bell_draw(own_key, dims, width, limit, pieces=(), held_as=jnp.bfloat16):
    values = jax.random.normal(own_key, dims, jnp.float32) * width
    if len(pieces) > 0:
        values = levels(own_key, dims, pieces, -0.22, 0.18) * values
    return jnp.clip(values, min=-limit, max=limit).astype(held_as)


def setup_inputs(seed: int = 0) -> dict:
    seeds = jax.random.split(jax.random.key(seed), 13)
    return {
        "queries": draw_queries(jax.random.fold_in(seeds[12], 71), 0),
        "key_value": draw_key_value(jax.random.fold_in(seeds[12], 71), 0),
        "mamba_in": bell_draw(seeds[2], (SECTIONS, SEQ, INNER), 1.0, 6.0, ((0, 8), (1, 32), (2, 4))),
        "gate_in": bell_draw(seeds[3], (SECTIONS, SEQ, INNER), 1.0, 6.0, ((0, 8), (1, 32), (2, 4))),
        "step_low": bell_draw(seeds[4], (SECTIONS, SEQ, STEP_RANK), 0.5, 3.0, ((0, 8), (1, 32))),
        "step_weight": bell_draw(seeds[5], (SECTIONS, STEP_RANK, INNER), STEP_RANK ** -0.5, 0.25, ((0, 8), (2, 4))),
        "step_bias": jnp.clip(-4.6 + 1.3999999 * jax.random.uniform(seeds[6], (SECTIONS, INNER), jnp.float32) ** levels(seeds[6], (SECTIONS, INNER), ((0, 8), (1, 4)), -0.2, 0.2), -4.6, -3.2),
        "decay_rate": draw_decay_rate(jax.random.fold_in(seeds[12], 71), 0),
        "conv_weight": bell_draw(seeds[8], (SECTIONS, CONV, INNER), 0.5, 3.0, ((0, 8), (2, 4)), jnp.float32),
        "conv_bias": bell_draw(seeds[9], (SECTIONS, INNER), 0.5, 3.0, ((0, 8), (1, 4)), jnp.float32),
        "state_weight": bell_draw(seeds[10], (SECTIONS, INNER, 2 * STATE), INNER ** -0.5, 0.0625, ((0, 8), (1, 4))),
        "skip_gain": jnp.clip(0.5 + 1.0 * jax.random.uniform(seeds[11], (SECTIONS, INNER), jnp.float32) ** levels(seeds[11], (SECTIONS, INNER), ((0, 8), (1, 4)), -0.2, 0.2), 0.5, 1.5),
    }


def attention_section(queries, key_value):
    group_size = Q_HEADS // KV_HEADS
    positions = jnp.arange(SEQ, dtype=jnp.int32)
    causal = positions[:, None] >= positions[None, :]

    def single_head(head):
        query_head = queries[:, head, :]
        key_head = key_value[0, :, head // group_size, :]
        value_head = key_value[1, :, head // group_size, :]
        scores = jnp.dot(query_head, key_head.T, preferred_element_type=jnp.float32) / math.sqrt(HEAD_DIM)
        scores = jnp.where(causal, scores, -jnp.inf)
        maximum = lax.optimization_barrier(jnp.max(scores, axis=1, keepdims=True))
        expterm = jnp.exp(scores - maximum)
        denominator = lax.optimization_barrier(jnp.sum(expterm, axis=1, keepdims=True))
        mixed = jnp.dot(expterm.astype(jnp.bfloat16), value_head, preferred_element_type=jnp.float32) / denominator
        return mixed.astype(jnp.bfloat16)
    heads_out = lax.map(single_head, jnp.arange(Q_HEADS, dtype=jnp.int32))
    return jnp.transpose(heads_out, (1, 0, 2))

def mamba_section(mamba_in, gate_in, step_low, step_weight, step_bias, decay_rate, conv_weight, conv_bias, state_weight, skip_gain):
    padded = jnp.concatenate([jnp.zeros((CONV - 1, INNER), jnp.float32), mamba_in.astype(jnp.float32)], axis=0)
    conv_out = conv_bias[None, :]
    for tap_index in range(CONV):
        conv_out = conv_out + conv_weight[tap_index][None, :] * padded[tap_index:tap_index + SEQ]
    inner_act = jax.nn.silu(conv_out).astype(jnp.bfloat16)
    entry_read = jnp.dot(inner_act, state_weight, preferred_element_type=jnp.float32)
    entry_map = entry_read[:, :STATE]
    read_map = entry_read[:, STATE:]
    step_size = jax.nn.softplus(jnp.dot(step_low, step_weight, preferred_element_type=jnp.float32) + step_bias[None, :])
    drive_input = step_size * inner_act.astype(jnp.float32)

    def advance(carry_state, row_data):
        step_row, drive_row, entry_row, read_row = row_data
        carry_state = jnp.exp(-decay_rate * step_row[None, :]) * carry_state + entry_row[:, None] * drive_row[None, :]
        return (carry_state, lax.optimization_barrier(jnp.sum(read_row[:, None] * carry_state, axis=0)))
    _, scanned = lax.scan(advance, jnp.zeros((STATE, INNER), jnp.float32), (step_size, drive_input, entry_map, read_map))
    scan_out = scanned + skip_gain[None, :] * inner_act.astype(jnp.float32)
    return (scan_out * jax.nn.silu(gate_in.astype(jnp.float32))).astype(jnp.bfloat16)

def attention_pair(pair):
    return attention_section(pair[0], pair[1])

def mamba_group(group):
    return mamba_section(*group)

def reference(queries, key_value, mamba_in, gate_in, step_low, step_weight, step_bias, decay_rate, conv_weight, conv_bias, state_weight, skip_gain):
    mixed = lax.map(attention_pair, (queries, key_value))
    gated = lax.map(mamba_group, (mamba_in, gate_in, step_low, step_weight, step_bias, decay_rate, conv_weight, conv_bias, state_weight, skip_gain))
    return (jnp.roll(mixed, 1, axis=0), jnp.roll(gated, 1, axis=0))
```

```python
import functools
import math

import jax
import jax.numpy as jnp
from jax import lax
from jax.experimental import pallas as pl
from jax.experimental.pallas import tpu as pltpu
from jax.sharding import Mesh, PartitionSpec as P

LOG2E = math.log2(math.e)
CTX = ("zh", "zc", "core")
HALO = 16
F32 = jnp.float32
BF16 = jnp.bfloat16
VMEM = pl.BlockSpec(memory_space=pltpu.VMEM)
SMEM = pl.BlockSpec(memory_space=pltpu.SMEM)


def kernel_call(body, out_shape, args, specs=None, scratch=(), flops=0, nbytes=0, limit=48):
    outs = out_shape if isinstance(out_shape, (tuple, list)) else (out_shape,)
    return pl.pallas_call(
        body,
        out_shape=out_shape,
        in_specs=specs or [VMEM] * len(args),
        out_specs=jax.tree.map(lambda _: VMEM, out_shape),
        scratch_shapes=list(scratch),
        compiler_params=pltpu.CompilerParams(vmem_limit_bytes=limit << 20),
        cost_estimate=pl.CostEstimate(flops=flops, bytes_accessed=nbytes, transcendentals=0),
    )(*args)


def step_body(low_ref, weight_ref, bias_ref, step_ref):
    cols = weight_ref.shape[1]
    width = 512
    for at in range(0, cols, width):
        v = jnp.dot(low_ref[...], weight_ref[:, at : at + width], preferred_element_type=F32)
        v = v + bias_ref[:, at : at + width]
        step_ref[:, at : at + width] = jnp.maximum(v, 0.0) + jnp.log1p(jnp.exp(-jnp.abs(v)))


def conv_body(x_ref, halo_ref, weight_ref, bias_ref, proj_ref, act_ref, read_ref):
    rows, cols = x_ref.shape
    taps = weight_ref.shape[0]
    width = 256
    total = jnp.zeros(read_ref.shape, F32)
    for at in range(0, cols, width):
        lanes = slice(at, at + width)
        padded = jnp.concatenate([halo_ref[:, lanes].astype(F32), x_ref[:, lanes].astype(F32)], axis=0)
        v = bias_ref[:, lanes]
        for tap in range(taps):
            first = HALO - (taps - 1) + tap
            v = v + weight_ref[tap : tap + 1, lanes] * padded[first : first + rows]
        act = (v / (1.0 + jnp.exp(-v))).astype(BF16)
        act_ref[:, lanes] = act
        total = total + lax.dot_general(
            act, proj_ref[:, lanes], (((1,), (1,)), ((), ())), preferred_element_type=F32
        )
    read_ref[...] = total


def wide(row, count):
    return jnp.broadcast_to(row, (count, row.shape[1]))


def local_body(step_ref, act_ref, entry_ref, rate_ref, out_ref, drive_ref):
    rows, cols = step_ref.shape
    count = rate_ref.shape[0]
    drive_ref[...] = step_ref[...] * act_ref[...].astype(F32)
    rate = rate_ref[...] * -LOG2E

    def block(at, carry):
        state, elapsed = carry
        base = pl.multiple_of(at * 16, 16)
        for i in range(16):
            step = wide(step_ref[pl.ds(base + i, 1), :], count)
            drive = wide(drive_ref[pl.ds(base + i, 1), :], count)
            entry = jnp.concatenate([entry_ref[base + i]] * (cols // 128), axis=1)
            state = jnp.exp2(rate * step) * state + entry * drive
            elapsed = elapsed + step
        return state, elapsed

    zero = jnp.zeros((count, cols), F32)
    state, elapsed = lax.fori_loop(0, rows // 16, block, (zero, zero))
    decay = jnp.exp2(rate * elapsed)
    half = count // 2
    for part in range(2 * cols // 128):
        lanes = slice(part // 2 * 128, part // 2 * 128 + 128)
        top = part % 2 * half
        both = jnp.concatenate([state[top : top + half, lanes], decay[top : top + half, lanes]], axis=0)
        out_ref[part] = both.astype(out_ref.dtype)


def prefix_body(in_ref, after_ref, out_ref):
    places, both, lanes = in_ref.shape
    half = both // 2
    state = jnp.zeros((half, lanes), F32)
    for place in range(places):
        out_ref[place] = state
        pair = in_ref[place].astype(F32)
        state = pair[half:] * state + pair[:half]


def scan_body(step_ref, act_ref, entry_ref, read_ref, rate_ref, enter_ref, skip_ref, gate_ref, after_ref, out_ref, drive_ref, held_ref):
    rows, cols = step_ref.shape
    count = rate_ref.shape[0]
    span = held_ref.shape[0] // count
    drive_ref[...] = step_ref[...] * act_ref[...].astype(F32)
    rate = rate_ref[...] * -LOG2E
    wanted = lax.broadcasted_iota(jnp.int32, (2 * count, span * count), 1) % count + count
    spread = (lax.broadcasted_iota(jnp.int32, wanted.shape, 0) == wanted).astype(BF16)
    held_at = lax.broadcasted_iota(jnp.int32, (span, span * count), 1) // count
    own = held_at == lax.broadcasted_iota(jnp.int32, held_at.shape, 0)
    state = jnp.concatenate(
        [
            jnp.concatenate([enter_ref[2 * block], enter_ref[2 * block + 1]], axis=0)
            for block in range(cols // 128)
        ],
        axis=1,
    )

    def chunk(at, state):
        base = pl.multiple_of(at * span, span)
        for i in range(0, span, 2):
            pair = []
            for j in (i, i + 1):
                step = wide(step_ref[pl.ds(base + j, 1), :], count)
                drive = wide(drive_ref[pl.ds(base + j, 1), :], count)
                entry = jnp.concatenate([entry_ref[base + j]] * (cols // 128), axis=1)
                state = jnp.exp2(rate * step) * state + entry * drive
                pair.append(state)
            held_ref[i * count : (i + 2) * count, :] = jnp.concatenate(pair, axis=0).astype(BF16)
        read = jnp.dot(read_ref[pl.ds(base, span), :].astype(BF16), spread, preferred_element_type=F32)
        read = jnp.where(own, read, 0.0).astype(BF16)
        width = 512
        for lane in range(0, cols, width):
            lanes = slice(lane, lane + width)
            scanned = jnp.dot(read, held_ref[:, lanes], preferred_element_type=F32)
            act = act_ref[pl.ds(base, span), lanes].astype(F32)
            gate = gate_ref[pl.ds(base, span), lanes].astype(F32)
            full = scanned + skip_ref[:, lanes] * act
            out_ref[pl.ds(base, span), lanes] = (full * (gate / (1.0 + jnp.exp(-gate)))).astype(out_ref.dtype)
        return state

    lax.fori_loop(0, rows // span, chunk, state)


def attend_body(place_ref, q_ref, kv_ref, after_ref, out_ref, held_ref, top_ref, acc_ref, *, slot, group):
    cores, slots, _, rows, width = kv_ref.shape[1:]
    zh, zc, core = place_ref[0], place_ref[1], place_ref[2]
    keys = cores * slots * rows
    scale = LOG2E / math.sqrt(width)
    tile = 128
    tiles = [slice(first, first + tile) for first in range(0, q_ref.shape[0], tile)]
    query_block = 2 * (zc ^ slot) + core

    def scores_of(at, lines):
        k = kv_ref[at, :, :, 0].reshape(keys, width)
        return lax.dot_general(q_ref[lines, :], k, (((1,), (1,)), ((), ())), preferred_element_type=F32)

    def folded(s):
        return functools.reduce(jnp.maximum, [s[:, lane : lane + width] for lane in range(0, keys, width)])

    for lines in tiles:
        s = scores_of(zh, lines)
        line = lax.broadcasted_iota(jnp.int32, s.shape, 0) + lines.start
        column = lax.broadcasted_iota(jnp.int32, s.shape, 1)
        query_pos = query_block * rows + line // group
        key_block = 2 * (zc ^ (column // rows % slots)) + column // (rows * slots)
        s = jnp.where(key_block * rows + column % rows <= query_pos, s, -jnp.inf)
        held_ref[zh, lines, :] = s
        top_ref[lines, :] = folded(s)

    def score(at, _):
        for lines in tiles:
            s = scores_of(at, lines)
            held_ref[at, lines, :] = s
            top_ref[lines, :] = jnp.maximum(top_ref[lines, :], folded(s))
        return 0

    lax.fori_loop(0, zh, score, 0)
    for lines in tiles:
        top = jnp.max(top_ref[lines, :], axis=1, keepdims=True) * scale
        top_ref[lines, :] = jnp.broadcast_to(top, (tile, width))
    acc_ref[...] = jnp.zeros_like(acc_ref)
    ones = jnp.ones((keys, width), BF16)

    def weigh(at, _):
        v = jnp.concatenate([kv_ref[at, :, :, 1].reshape(keys, width), ones], axis=1)
        for lines in tiles:
            s, top = held_ref[at, lines, :], top_ref[lines, :]
            p = jnp.concatenate(
                [jnp.exp2(s[:, lane : lane + width] * scale - top).astype(BF16) for lane in range(0, keys, width)],
                axis=1,
            )
            acc_ref[lines, :] += jnp.dot(p, v, preferred_element_type=F32)
        return 0

    lax.fori_loop(0, zh + 1, weigh, 0)
    out_ref[...] = (acc_ref[:, :width] / acc_ref[:, width:]).astype(out_ref.dtype)


def per_device(
    queries,
    key_value,
    mamba_in,
    gate_in,
    step_low,
    step_weight,
    step_bias,
    decay_rate,
    conv_weight,
    conv_bias,
    state_weight,
    skip_gain,
):
    queries, key_value, mamba_in, gate_in = queries[0], key_value[0], mamba_in[0], gate_in[0]
    decay_rate, state_weight = decay_rate[0], state_weight[0]
    rows, heads, width = queries.shape
    kv_heads = key_value.shape[2]
    group = heads // kv_heads
    cols = mamba_in.shape[1]
    count = decay_rate.shape[0]
    taps = conv_weight.shape[1]
    pipes = lax.axis_size("pipe")
    places = lax.axis_size(CTX)
    zh, zc, core = (lax.axis_index(a) for a in CTX)
    swap = [(0, 1), (1, 0)]

    own_kv = lax.dynamic_index_in_dim(key_value, zc, 2, False)
    other_kv = lax.ppermute(lax.dynamic_index_in_dim(key_value, 1 - zc, 2, False), "zc", swap)
    halo = lax.ppermute(mamba_in[rows - HALO :], CTX, [(i, i + 1) for i in range(places - 1)])
    own_kv, other_kv, halo = lax.optimization_barrier((own_kv, other_kv, halo))
    kv = lax.all_gather(jnp.stack([own_kv, other_kv]), ("zh", "core"))
    kv = kv.reshape((lax.axis_size("zh"), lax.axis_size("core")) + kv.shape[1:])

    step = kernel_call(
        step_body,
        jax.ShapeDtypeStruct((rows, cols), F32),
        (step_low[0], step_weight[0], step_bias),
        flops=2 * rows * cols * step_low.shape[2],
        nbytes=4 << 20,
    )
    act, partial = kernel_call(
        conv_body,
        (jax.ShapeDtypeStruct((rows, cols), BF16), jax.ShapeDtypeStruct((rows, 2 * count), F32)),
        (mamba_in, halo, conv_weight[0], conv_bias, state_weight.T),
        nbytes=4 << 20,
    )
    entry_read = lax.psum(partial, "tp")
    queries, entry_read = lax.optimization_barrier((queries, entry_read))
    grouped = queries.reshape(rows, kv_heads, group, width)
    own_q = lax.dynamic_index_in_dim(grouped, zc, 1, False)
    other_q = lax.ppermute(lax.dynamic_index_in_dim(grouped, 1 - zc, 1, False), "zc", swap)
    place = jnp.stack([zh, zc, core]).astype(jnp.int32)

    entry = jnp.broadcast_to(entry_read[:, :count, None], (rows, count, 128))
    span = 32
    parts = kernel_call(
        local_body,
        jax.ShapeDtypeStruct((2 * cols // 128, count, 128), BF16),
        (step, act, entry, decay_rate),
        scratch=[pltpu.VMEM((rows, cols), F32)],
        nbytes=16 << 20,
    )
    parts = lax.all_to_all(parts, CTX, 0, 0, tiled=True)
    entering = kernel_call(
        prefix_body, jax.ShapeDtypeStruct((places, count // 2, 128), F32), (parts, other_q), nbytes=1 << 20
    )
    entering = lax.all_to_all(entering, CTX, 0, 0, tiled=True)
    def attend(q, slot, after):
        lines = rows * group
        keys = 4 * rows
        return kernel_call(
            functools.partial(attend_body, slot=slot, group=group),
            jax.ShapeDtypeStruct((lines, width), BF16),
            (place, q.reshape(lines, width), kv, after),
            specs=[SMEM, VMEM, VMEM, SMEM if after is place else VMEM],
            scratch=[
                pltpu.VMEM((places // 4, lines, keys), F32),
                pltpu.VMEM((lines, width), F32),
                pltpu.VMEM((lines, 2 * width), F32),
            ],
            flops=4 * lines * width * rows * places,
            nbytes=16 << 20,
        ).reshape(rows, group, width)

    far = attend(other_q, 1, place)
    far_sent = lax.ppermute(
        far,
        ("pipe", "zc"),
        [(2 * i + j, 2 * ((i + 1) % pipes) + 1 - j) for i in range(pipes) for j in range(2)],
    )
    gated = kernel_call(
        scan_body,
        jax.ShapeDtypeStruct((rows, cols), BF16),
        (step, act, entry, entry_read, decay_rate, entering, skip_gain, gate_in, far),

        scratch=[pltpu.VMEM((rows, cols), F32), pltpu.VMEM((span * count, cols), BF16)],
        nbytes=16 << 20,
    )
    mamba_out = lax.ppermute(gated, "pipe", [(i, (i + 1) % pipes) for i in range(pipes)])
    near = attend(own_q, 0, far_sent)
    near = lax.ppermute(near, "pipe", [(i, (i + 1) % pipes) for i in range(pipes)])
    far = far_sent
    first = jnp.where(zc == 0, near, far)
    second = jnp.where(zc == 0, far, near)
    attended = jnp.concatenate([first, second], axis=1)
    return (attended[None], mamba_out[None])


def solution(mesh):
    pipes, places, parts = mesh.devices.shape
    split = Mesh(
        mesh.devices.reshape(pipes, places // 4, 2, 2, parts), ("pipe", "zh", "zc", "core", "tp")
    )
    return jax.shard_map(
        per_device,
        mesh=split,
        in_specs=(
            P("pipe", CTX, "tp", None),
            P("pipe", None, CTX, "tp", None),
            P("pipe", CTX, "tp"),
            P("pipe", CTX, "tp"),
            P("pipe", CTX, None),
            P("pipe", None, "tp"),
            P("pipe", "tp"),
            P("pipe", None, "tp"),
            P("pipe", None, "tp"),
            P("pipe", "tp"),
            P("pipe", "tp", None),
            P("pipe", "tp"),
        ),
        out_specs=(P("pipe", CTX, "tp", None), P("pipe", CTX, "tp")),
        check_vma=False,
    )
```

```python
import functools
import math

import jax
import jax.numpy as jnp
from jax import lax
from jax.experimental import pallas as pl
from jax.experimental.pallas import tpu as pltpu
from jax.sharding import Mesh, PartitionSpec as P

LOG2E = math.log2(math.e)
CTX = ("zh", "zc", "core")
HALO = 16
F32 = jnp.float32
BF16 = jnp.bfloat16
VMEM = pl.BlockSpec(memory_space=pltpu.VMEM)
SMEM = pl.BlockSpec(memory_space=pltpu.SMEM)


def kernel_call(body, out_shape, args, specs=None, scratch=(), flops=0, nbytes=0, limit=48):
    outs = out_shape if isinstance(out_shape, (tuple, list)) else (out_shape,)
    return pl.pallas_call(
        body,
        out_shape=out_shape,
        in_specs=specs or [VMEM] * len(args),
        out_specs=jax.tree.map(lambda _: VMEM, out_shape),
        scratch_shapes=list(scratch),
        compiler_params=pltpu.CompilerParams(vmem_limit_bytes=limit << 20),
        cost_estimate=pl.CostEstimate(flops=flops, bytes_accessed=nbytes, transcendentals=0),
    )(*args)


def step_body(low_ref, weight_ref, bias_ref, after_ref, step_ref):
    cols = weight_ref.shape[1]
    width = 512
    for at in range(0, cols, width):
        v = jnp.dot(low_ref[...], weight_ref[:, at : at + width], preferred_element_type=F32)
        v = v + bias_ref[:, at : at + width]
        step_ref[:, at : at + width] = jnp.maximum(v, 0.0) + jnp.log1p(jnp.exp(-jnp.abs(v)))


def conv_body(x_ref, halo_ref, weight_ref, bias_ref, proj_ref, act_ref, read_ref):
    rows, cols = x_ref.shape
    taps = weight_ref.shape[0]
    width = 256
    total = jnp.zeros(read_ref.shape[1:], F32)
    for at in range(0, cols, width):
        lanes = slice(at, at + width)
        padded = jnp.concatenate([halo_ref[:, lanes].astype(F32), x_ref[:, lanes].astype(F32)], axis=0)
        v = bias_ref[:, lanes]
        for tap in range(taps):
            first = HALO - (taps - 1) + tap
            v = v + weight_ref[tap : tap + 1, lanes] * padded[first : first + rows]
        act = (v / (1.0 + jnp.exp(-v))).astype(BF16)
        act_ref[:, lanes] = act
        total = total + lax.dot_general(
            proj_ref[:, lanes], act, (((1,), (1,)), ((), ())), preferred_element_type=F32
        )
    for part in range(read_ref.shape[0]):
        read_ref[part] = total


def wide(row, count):
    return jnp.broadcast_to(row, (count, row.shape[1]))


def spread_entry(maps_ref, entry_ref):
    maps = functools.reduce(jnp.add, [maps_ref[part] for part in range(maps_ref.shape[0])])
    rows, count, lanes = entry_ref.shape
    for row in range(rows):
        entry_ref[row] = jnp.broadcast_to(maps[:count, row : row + 1], (count, lanes))
    return maps


def local_body(step_ref, act_ref, maps_ref, rate_ref, out_ref, drive_ref, entry_ref):
    rows, cols = step_ref.shape
    count = rate_ref.shape[0]
    drive_ref[...] = step_ref[...] * act_ref[...].astype(F32)
    spread_entry(maps_ref, entry_ref)
    rate = rate_ref[...] * -LOG2E

    def block(at, carry):
        state, elapsed = carry
        base = pl.multiple_of(at * 16, 16)
        for i in range(16):
            step = wide(step_ref[pl.ds(base + i, 1), :], count)
            drive = wide(drive_ref[pl.ds(base + i, 1), :], count)
            entry = jnp.concatenate([entry_ref[base + i]] * (cols // 128), axis=1)
            state = jnp.exp2(rate * step) * state + entry * drive
            elapsed = elapsed + step
        return state, elapsed

    zero = jnp.zeros((count, cols), F32)
    state, elapsed = lax.fori_loop(0, rows // 16, block, (zero, zero))
    decay = jnp.exp2(rate * elapsed)
    half = count // 2
    for part in range(2 * cols // 128):
        lanes = slice(part // 2 * 128, part // 2 * 128 + 128)
        top = part % 2 * half
        both = jnp.concatenate([state[top : top + half, lanes], decay[top : top + half, lanes]], axis=0)
        out_ref[part] = both.astype(out_ref.dtype)


def prefix_body(in_ref, after_ref, out_ref):
    places, both, lanes = in_ref.shape
    half = both // 2
    state = jnp.zeros((half, lanes), F32)
    for place in range(places):
        out_ref[place] = state
        pair = in_ref[place].astype(F32)
        state = pair[half:] * state + pair[:half]


def scan_body(
    step_ref, act_ref, maps_ref, rate_ref, enter_ref, skip_ref, gate_ref, out_ref,
    drive_ref, entry_ref, read_ref, held_ref,
):
    rows, cols = step_ref.shape
    count = rate_ref.shape[0]
    span = held_ref.shape[0] // count
    drive_ref[...] = step_ref[...] * act_ref[...].astype(F32)
    rate = rate_ref[...] * -LOG2E
    maps = spread_entry(maps_ref, entry_ref)
    shape = (count, span * count)
    spread = (lax.broadcasted_iota(jnp.int32, shape, 0) == lax.broadcasted_iota(jnp.int32, shape, 1) % count)
    read = jnp.dot(maps[count:].T.astype(BF16), spread.astype(BF16), preferred_element_type=F32)
    held_at = lax.broadcasted_iota(jnp.int32, read.shape, 1) // count
    own = held_at == lax.broadcasted_iota(jnp.int32, read.shape, 0) % span
    read_ref[...] = jnp.where(own, read, 0.0).astype(BF16)
    state = jnp.concatenate(
        [
            jnp.concatenate([enter_ref[2 * block], enter_ref[2 * block + 1]], axis=0)
            for block in range(cols // 128)
        ],
        axis=1,
    )

    def chunk(at, state):
        base = pl.multiple_of(at * span, span)
        for i in range(0, span, 2):
            pair = []
            for j in (i, i + 1):
                step = wide(step_ref[pl.ds(base + j, 1), :], count)
                drive = wide(drive_ref[pl.ds(base + j, 1), :], count)
                entry = jnp.concatenate([entry_ref[base + j]] * (cols // 128), axis=1)
                state = jnp.exp2(rate * step) * state + entry * drive
                pair.append(state)
            held_ref[i * count : (i + 2) * count, :] = jnp.concatenate(pair, axis=0).astype(BF16)
        read = read_ref[pl.ds(base, span), :]
        width = 512
        for lane in range(0, cols, width):
            lanes = slice(lane, lane + width)
            scanned = jnp.dot(read, held_ref[:, lanes], preferred_element_type=F32)
            act = act_ref[pl.ds(base, span), lanes].astype(F32)
            gate = gate_ref[pl.ds(base, span), lanes].astype(F32)
            full = scanned + skip_ref[:, lanes] * act
            out_ref[pl.ds(base, span), lanes] = (full * (gate / (1.0 + jnp.exp(-gate)))).astype(out_ref.dtype)
        return state

    lax.fori_loop(0, rows // span, chunk, state)


def attend_body(place_ref, q_ref, kv_ref, after_ref, out_ref, held_ref, top_ref, acc_ref, *, slot, group):
    cores, slots, _, rows, width = kv_ref.shape[1:]
    zh, zc, core = place_ref[0], place_ref[1], place_ref[2]
    keys = cores * slots * rows
    scale = LOG2E / math.sqrt(width)
    tile = 128
    tiles = [slice(first, first + tile) for first in range(0, q_ref.shape[0], tile)]
    query_block = 2 * (zc ^ slot) + core

    def scores_of(at, lines):
        k = kv_ref[at, :, :, 0].reshape(keys, width)
        return lax.dot_general(q_ref[lines, :], k, (((1,), (1,)), ((), ())), preferred_element_type=F32)

    def folded(s):
        return functools.reduce(jnp.maximum, [s[:, lane : lane + width] for lane in range(0, keys, width)])

    for lines in tiles:
        s = scores_of(zh, lines)
        line = lax.broadcasted_iota(jnp.int32, s.shape, 0) + lines.start
        column = lax.broadcasted_iota(jnp.int32, s.shape, 1)
        query_pos = query_block * rows + line // group
        key_block = 2 * (zc ^ (column // rows % slots)) + column // (rows * slots)
        s = jnp.where(key_block * rows + column % rows <= query_pos, s, -jnp.inf)
        held_ref[zh, lines, :] = s
        top_ref[lines, :] = folded(s)

    def score(at, _):
        for lines in tiles:
            s = scores_of(at, lines)
            held_ref[at, lines, :] = s
            top_ref[lines, :] = jnp.maximum(top_ref[lines, :], folded(s))
        return 0

    lax.fori_loop(0, zh, score, 0)
    for lines in tiles:
        top = jnp.max(top_ref[lines, :], axis=1, keepdims=True) * scale
        top_ref[lines, :] = jnp.broadcast_to(top, (tile, width))
    acc_ref[...] = jnp.zeros_like(acc_ref)
    ones = jnp.ones((keys, width), BF16)

    def weigh(at, _):
        v = jnp.concatenate([kv_ref[at, :, :, 1].reshape(keys, width), ones], axis=1)
        for lines in tiles:
            s, top = held_ref[at, lines, :], top_ref[lines, :]
            p = jnp.concatenate(
                [jnp.exp2(s[:, lane : lane + width] * scale - top).astype(BF16) for lane in range(0, keys, width)],
                axis=1,
            )
            acc_ref[lines, :] += jnp.dot(p, v, preferred_element_type=F32)
        return 0

    lax.fori_loop(0, zh + 1, weigh, 0)
    out_ref[...] = (acc_ref[:, :width] / acc_ref[:, width:]).astype(out_ref.dtype)


def per_device(
    queries,
    key_value,
    mamba_in,
    gate_in,
    step_low,
    step_weight,
    step_bias,
    decay_rate,
    conv_weight,
    conv_bias,
    state_weight,
    skip_gain,
):
    queries, key_value, mamba_in, gate_in = queries[0], key_value[0], mamba_in[0], gate_in[0]
    decay_rate, state_weight = decay_rate[0], state_weight[0]
    rows, heads, width = queries.shape
    kv_heads = key_value.shape[2]
    group = heads // kv_heads
    cols = mamba_in.shape[1]
    count = decay_rate.shape[0]
    parts_tp = lax.axis_size("tp")
    pipes = lax.axis_size("pipe")
    places = lax.axis_size(CTX)
    zh, zc, core = (lax.axis_index(a) for a in CTX)
    swap = [(0, 1), (1, 0)]

    own_kv = lax.dynamic_index_in_dim(key_value, zc, 2, False)
    other_kv = lax.ppermute(lax.dynamic_index_in_dim(key_value, 1 - zc, 2, False), "zc", swap)
    halo = lax.ppermute(mamba_in[rows - HALO :], CTX, [(i, i + 1) for i in range(places - 1)])
    own_kv, other_kv, halo = lax.optimization_barrier((own_kv, other_kv, halo))
    kv = lax.all_gather(jnp.stack([own_kv, other_kv]), ("zh", "core"))
    kv = kv.reshape((lax.axis_size("zh"), lax.axis_size("core")) + kv.shape[1:])

    act, partial = kernel_call(
        conv_body,
        (jax.ShapeDtypeStruct((rows, cols), BF16), jax.ShapeDtypeStruct((parts_tp, 2 * count, rows), F32)),
        (mamba_in, halo, conv_weight[0], conv_bias, state_weight.T),
        nbytes=4 << 20,
    )
    queries, _ = lax.optimization_barrier((queries, act))
    grouped = queries.reshape(rows, kv_heads, group, width)
    own_q = lax.dynamic_index_in_dim(grouped, zc, 1, False)
    other_q = lax.ppermute(lax.dynamic_index_in_dim(grouped, 1 - zc, 1, False), "zc", swap)
    place = jnp.stack([zh, zc, core]).astype(jnp.int32)

    step = kernel_call(
        step_body,
        jax.ShapeDtypeStruct((rows, cols), F32),
        (step_low[0], step_weight[0], step_bias, act),
        flops=2 * rows * cols * step_low.shape[2],
        nbytes=4 << 20,
    )
    maps = lax.all_to_all(partial, "tp", 0, 0, tiled=True)
    span = 32
    parts = kernel_call(
        local_body,
        jax.ShapeDtypeStruct((2 * cols // 128, count, 128), BF16),
        (step, act, maps, decay_rate),
        scratch=[pltpu.VMEM((rows, cols), F32), pltpu.VMEM((rows, count, 128), F32)],
        nbytes=16 << 20,
    )
    parts = lax.all_to_all(parts, CTX, 0, 0, tiled=True)
    entering = kernel_call(
        prefix_body, jax.ShapeDtypeStruct((places, count // 2, 128), F32), (parts, other_q), nbytes=1 << 20
    )
    entering = lax.all_to_all(entering, CTX, 0, 0, tiled=True)
    def attend(q, slot, after):
        lines = rows * group
        keys = 4 * rows
        return kernel_call(
            functools.partial(attend_body, slot=slot, group=group),
            jax.ShapeDtypeStruct((lines, width), BF16),
            (place, q.reshape(lines, width), kv, after),
            specs=[SMEM, VMEM, VMEM, VMEM],
            scratch=[
                pltpu.VMEM((places // 4, lines, keys), F32),
                pltpu.VMEM((lines, width), F32),
                pltpu.VMEM((lines, 2 * width), F32),
            ],
            flops=4 * lines * width * rows * places,
            nbytes=16 << 20,
        ).reshape(rows, group, width)

    gated = kernel_call(
        scan_body,
        jax.ShapeDtypeStruct((rows, cols), BF16),
        (step, act, maps, decay_rate, entering, skip_gain, gate_in),

        scratch=[
            pltpu.VMEM((rows, cols), F32),
            pltpu.VMEM((rows, count, 128), F32),
            pltpu.VMEM((rows, span * count), BF16),
            pltpu.VMEM((span * count, cols), BF16),
        ],
        nbytes=16 << 20,
    )
    mamba_out = lax.ppermute(gated, "pipe", [(i, (i + 1) % pipes) for i in range(pipes)])
    far = attend(other_q, 1, gated)
    far_sent = lax.ppermute(
        far,
        ("pipe", "zc"),
        [(2 * i + j, 2 * ((i + 1) % pipes) + 1 - j) for i in range(pipes) for j in range(2)],
    )
    near = attend(own_q, 0, gated)
    near = lax.ppermute(near, "pipe", [(i, (i + 1) % pipes) for i in range(pipes)])
    far = far_sent
    first = jnp.where(zc == 0, near, far)
    second = jnp.where(zc == 0, far, near)
    attended = jnp.concatenate([first, second], axis=1)
    return (attended[None], mamba_out[None])


def solution(mesh):
    pipes, places, parts = mesh.devices.shape
    split = Mesh(
        mesh.devices.reshape(pipes, places // 4, 2, 2, parts), ("pipe", "zh", "zc", "core", "tp")
    )
    return jax.shard_map(
        per_device,
        mesh=split,
        in_specs=(
            P("pipe", CTX, "tp", None),
            P("pipe", None, CTX, "tp", None),
            P("pipe", CTX, "tp"),
            P("pipe", CTX, "tp"),
            P("pipe", CTX, None),
            P("pipe", None, "tp"),
            P("pipe", "tp"),
            P("pipe", None, "tp"),
            P("pipe", None, "tp"),
            P("pipe", "tp"),
            P("pipe", "tp", None),
            P("pipe", "tp"),
        ),
        out_specs=(P("pipe", CTX, "tp", None), P("pipe", CTX, "tp")),
        check_vma=False,
    )
```

```python
import functools
import math

import jax
import jax.numpy as jnp
from jax import lax
from jax.experimental import pallas as pl
from jax.experimental.pallas import tpu as pltpu
from jax.sharding import Mesh, PartitionSpec as P

LOG2E = math.log2(math.e)
CTX = ("zh", "zc", "core")
HALO = 16
F32 = jnp.float32
BF16 = jnp.bfloat16
VMEM = pl.BlockSpec(memory_space=pltpu.VMEM)
SMEM = pl.BlockSpec(memory_space=pltpu.SMEM)


def kernel_call(body, out_shape, args, specs=None, scratch=(), flops=0, nbytes=0, limit=48):
    outs = out_shape if isinstance(out_shape, (tuple, list)) else (out_shape,)
    return pl.pallas_call(
        body,
        out_shape=out_shape,
        in_specs=specs or [VMEM] * len(args),
        out_specs=jax.tree.map(lambda _: VMEM, out_shape),
        scratch_shapes=list(scratch),
        compiler_params=pltpu.CompilerParams(vmem_limit_bytes=limit << 20),
        cost_estimate=pl.CostEstimate(flops=flops, bytes_accessed=nbytes, transcendentals=0),
    )(*args)


def step_body(low_ref, weight_ref, bias_ref, after_ref, step_ref):
    cols = weight_ref.shape[1]
    width = 512
    for at in range(0, cols, width):
        v = jnp.dot(low_ref[...], weight_ref[:, at : at + width], preferred_element_type=F32)
        v = v + bias_ref[:, at : at + width]
        step_ref[:, at : at + width] = jnp.maximum(v, 0.0) + jnp.log1p(jnp.exp(-jnp.abs(v)))


def conv_body(x_ref, halo_ref, weight_ref, bias_ref, proj_ref, act_ref, read_ref):
    rows, cols = x_ref.shape
    taps = weight_ref.shape[0]
    width = 256
    total = jnp.zeros(read_ref.shape[1:], F32)
    for at in range(0, cols, width):
        lanes = slice(at, at + width)
        padded = jnp.concatenate([halo_ref[:, lanes].astype(F32), x_ref[:, lanes].astype(F32)], axis=0)
        v = bias_ref[:, lanes]
        for tap in range(taps):
            first = HALO - (taps - 1) + tap
            v = v + weight_ref[tap : tap + 1, lanes] * padded[first : first + rows]
        act = (v / (1.0 + jnp.exp(-v))).astype(BF16)
        act_ref[:, lanes] = act
        total = total + lax.dot_general(
            proj_ref[:, lanes], act, (((1,), (1,)), ((), ())), preferred_element_type=F32
        )
    for part in range(read_ref.shape[0]):
        read_ref[part] = total


def wide(row, count):
    return jnp.broadcast_to(row, (count, row.shape[1]))


def spread_entry(maps_ref, entry_ref):
    maps = functools.reduce(jnp.add, [maps_ref[part] for part in range(maps_ref.shape[0])])
    rows, count, lanes = entry_ref.shape
    for row in range(rows):
        entry_ref[row] = jnp.broadcast_to(maps[:count, row : row + 1], (count, lanes))
    return maps


def local_body(step_ref, act_ref, maps_ref, rate_ref, out_ref, drive_ref, entry_ref):
    rows, cols = step_ref.shape
    count = rate_ref.shape[0]
    drive_ref[...] = step_ref[...] * act_ref[...].astype(F32)
    spread_entry(maps_ref, entry_ref)
    rate = rate_ref[...] * -LOG2E

    def block(at, carry):
        state, elapsed = carry
        base = pl.multiple_of(at * 16, 16)
        for i in range(16):
            step = wide(step_ref[pl.ds(base + i, 1), :], count)
            drive = wide(drive_ref[pl.ds(base + i, 1), :], count)
            entry = jnp.concatenate([entry_ref[base + i]] * (cols // 128), axis=1)
            state = jnp.exp2(rate * step) * state + entry * drive
            elapsed = elapsed + step
        return state, elapsed

    zero = jnp.zeros((count, cols), F32)
    state, elapsed = lax.fori_loop(0, rows // 16, block, (zero, zero))
    decay = jnp.exp2(rate * elapsed)
    half = count // 2
    for part in range(2 * cols // 128):
        lanes = slice(part // 2 * 128, part // 2 * 128 + 128)
        top = part % 2 * half
        both = jnp.concatenate([state[top : top + half, lanes], decay[top : top + half, lanes]], axis=0)
        out_ref[part] = both.astype(out_ref.dtype)


def prefix_body(in_ref, out_ref):
    places, both, lanes = in_ref.shape
    half = both // 2
    state = jnp.zeros((half, lanes), F32)
    for place in range(places):
        out_ref[place] = state
        pair = in_ref[place].astype(F32)
        state = pair[half:] * state + pair[:half]


def read_body(maps_ref, asked_ref, after_ref, out_ref):
    count = maps_ref.shape[1] // 2
    shape = (count, out_ref.shape[1])
    maps = functools.reduce(jnp.add, [maps_ref[part, count:] for part in range(maps_ref.shape[0])])
    spread = lax.broadcasted_iota(jnp.int32, shape, 0) == lax.broadcasted_iota(jnp.int32, shape, 1) % count
    read = jnp.dot(maps.T.astype(BF16), spread.astype(BF16), preferred_element_type=F32)
    held_at = lax.broadcasted_iota(jnp.int32, read.shape, 1) // count
    own = held_at == lax.broadcasted_iota(jnp.int32, read.shape, 0) % (shape[1] // count)
    out_ref[...] = jnp.where(own, read, 0.0).astype(BF16)


def scan_body(
    step_ref, act_ref, maps_ref, read_ref, rate_ref, enter_ref, skip_ref, gate_ref, out_ref,
    drive_ref, entry_ref, held_ref,
):
    rows, cols = step_ref.shape
    count = rate_ref.shape[0]
    span = held_ref.shape[0] // count
    drive_ref[...] = step_ref[...] * act_ref[...].astype(F32)
    rate = rate_ref[...] * -LOG2E
    spread_entry(maps_ref, entry_ref)
    state = jnp.concatenate(
        [
            jnp.concatenate([enter_ref[2 * block], enter_ref[2 * block + 1]], axis=0)
            for block in range(cols // 128)
        ],
        axis=1,
    )

    def chunk(at, state):
        base = pl.multiple_of(at * span, span)
        for i in range(0, span, 2):
            pair = []
            for j in (i, i + 1):
                step = wide(step_ref[pl.ds(base + j, 1), :], count)
                drive = wide(drive_ref[pl.ds(base + j, 1), :], count)
                entry = jnp.concatenate([entry_ref[base + j]] * (cols // 128), axis=1)
                state = jnp.exp2(rate * step) * state + entry * drive
                pair.append(state)
            held_ref[i * count : (i + 2) * count, :] = jnp.concatenate(pair, axis=0).astype(BF16)
        read = read_ref[pl.ds(base, span), :]
        width = 512
        for lane in range(0, cols, width):
            lanes = slice(lane, lane + width)
            scanned = jnp.dot(read, held_ref[:, lanes], preferred_element_type=F32)
            act = act_ref[pl.ds(base, span), lanes].astype(F32)
            gate = gate_ref[pl.ds(base, span), lanes].astype(F32)
            full = scanned + skip_ref[:, lanes] * act
            out_ref[pl.ds(base, span), lanes] = (full * (gate / (1.0 + jnp.exp(-gate)))).astype(out_ref.dtype)
        return state

    lax.fori_loop(0, rows // span, chunk, state)


def attend_body(place_ref, q_ref, kv_ref, after_ref, out_ref, held_ref, top_ref, acc_ref, *, slot, group):
    cores, slots, _, rows, width = kv_ref.shape[1:]
    zh, zc, core = place_ref[0], place_ref[1], place_ref[2]
    keys = cores * slots * rows
    scale = LOG2E / math.sqrt(width)
    tile = 128
    tiles = [slice(first, first + tile) for first in range(0, q_ref.shape[0], tile)]
    query_block = 2 * (zc ^ slot) + core

    def scores_of(at, lines):
        k = kv_ref[at, :, :, 0].reshape(keys, width)
        return lax.dot_general(q_ref[lines, :], k, (((1,), (1,)), ((), ())), preferred_element_type=F32)

    def folded(s):
        return functools.reduce(jnp.maximum, [s[:, lane : lane + width] for lane in range(0, keys, width)])

    for lines in tiles:
        s = scores_of(zh, lines)
        line = lax.broadcasted_iota(jnp.int32, s.shape, 0) + lines.start
        column = lax.broadcasted_iota(jnp.int32, s.shape, 1)
        query_pos = query_block * rows + line // group
        key_block = 2 * (zc ^ (column // rows % slots)) + column // (rows * slots)
        s = jnp.where(key_block * rows + column % rows <= query_pos, s, -jnp.inf)
        held_ref[zh, lines, :] = s
        top_ref[lines, :] = folded(s)

    def score(at, _):
        for lines in tiles:
            s = scores_of(at, lines)
            held_ref[at, lines, :] = s
            top_ref[lines, :] = jnp.maximum(top_ref[lines, :], folded(s))
        return 0

    lax.fori_loop(0, zh, score, 0)
    for lines in tiles:
        top = jnp.max(top_ref[lines, :], axis=1, keepdims=True) * scale
        top_ref[lines, :] = jnp.broadcast_to(top, (tile, width))
    acc_ref[...] = jnp.zeros_like(acc_ref)
    ones = jnp.ones((keys, width), BF16)

    def weigh(at, _):
        v = jnp.concatenate([kv_ref[at, :, :, 1].reshape(keys, width), ones], axis=1)
        for lines in tiles:
            s, top = held_ref[at, lines, :], top_ref[lines, :]
            p = jnp.concatenate(
                [jnp.exp2(s[:, lane : lane + width] * scale - top).astype(BF16) for lane in range(0, keys, width)],
                axis=1,
            )
            acc_ref[lines, :] += jnp.dot(p, v, preferred_element_type=F32)
        return 0

    lax.fori_loop(0, zh + 1, weigh, 0)
    out_ref[...] = (acc_ref[:, :width] / acc_ref[:, width:]).astype(out_ref.dtype)


def per_device(
    queries,
    key_value,
    mamba_in,
    gate_in,
    step_low,
    step_weight,
    step_bias,
    decay_rate,
    conv_weight,
    conv_bias,
    state_weight,
    skip_gain,
):
    queries, key_value, mamba_in, gate_in = queries[0], key_value[0], mamba_in[0], gate_in[0]
    decay_rate, state_weight = decay_rate[0], state_weight[0]
    rows, heads, width = queries.shape
    kv_heads = key_value.shape[2]
    group = heads // kv_heads
    cols = mamba_in.shape[1]
    count = decay_rate.shape[0]
    parts_tp = lax.axis_size("tp")
    pipes = lax.axis_size("pipe")
    places = lax.axis_size(CTX)
    zh, zc, core = (lax.axis_index(a) for a in CTX)
    swap = [(0, 1), (1, 0)]

    own_kv = lax.dynamic_index_in_dim(key_value, zc, 2, False)
    other_kv = lax.ppermute(lax.dynamic_index_in_dim(key_value, 1 - zc, 2, False), "zc", swap)
    halo = lax.ppermute(mamba_in[rows - HALO :], CTX, [(i, i + 1) for i in range(places - 1)])
    own_kv, other_kv, halo = lax.optimization_barrier((own_kv, other_kv, halo))
    kv = lax.all_gather(jnp.stack([own_kv, other_kv]), ("zh", "core"))
    kv = kv.reshape((lax.axis_size("zh"), lax.axis_size("core")) + kv.shape[1:])

    act, partial = kernel_call(
        conv_body,
        (jax.ShapeDtypeStruct((rows, cols), BF16), jax.ShapeDtypeStruct((parts_tp, 2 * count, rows), F32)),
        (mamba_in, halo, conv_weight[0], conv_bias, state_weight.T),
        nbytes=4 << 20,
    )
    step = kernel_call(
        step_body,
        jax.ShapeDtypeStruct((rows, cols), F32),
        (step_low[0], step_weight[0], step_bias, act),
        flops=2 * rows * cols * step_low.shape[2],
        nbytes=4 << 20,
    )
    maps = lax.all_to_all(partial, "tp", 0, 0, tiled=True)
    queries, maps = lax.optimization_barrier((queries, maps))
    grouped = queries.reshape(rows, kv_heads, group, width)
    own_q = lax.dynamic_index_in_dim(grouped, zc, 1, False)
    other_q = lax.ppermute(lax.dynamic_index_in_dim(grouped, 1 - zc, 1, False), "zc", swap)
    place = jnp.stack([zh, zc, core]).astype(jnp.int32)

    span = 32
    parts = kernel_call(
        local_body,
        jax.ShapeDtypeStruct((2 * cols // 128, count, 128), BF16),
        (step, act, maps, decay_rate),
        scratch=[pltpu.VMEM((rows, cols), F32), pltpu.VMEM((rows, count, 128), F32)],
        nbytes=16 << 20,
    )
    parts = lax.all_to_all(parts, CTX, 0, 0, tiled=True)
    entering = kernel_call(
        prefix_body, jax.ShapeDtypeStruct((places, count // 2, 128), F32), (parts,), nbytes=1 << 20
    )
    read = kernel_call(
        read_body,
        jax.ShapeDtypeStruct((rows, span * count), BF16),
        (maps, entering, other_q),
        nbytes=1 << 20,
    )
    entering = lax.all_to_all(entering, CTX, 0, 0, tiled=True)
    def attend(q, slot, after):
        lines = rows * group
        keys = 4 * rows
        return kernel_call(
            functools.partial(attend_body, slot=slot, group=group),
            jax.ShapeDtypeStruct((lines, width), BF16),
            (place, q.reshape(lines, width), kv, after),
            specs=[SMEM, VMEM, VMEM, VMEM],
            scratch=[
                pltpu.VMEM((places // 4, lines, keys), F32),
                pltpu.VMEM((lines, width), F32),
                pltpu.VMEM((lines, 2 * width), F32),
            ],
            flops=4 * lines * width * rows * places,
            nbytes=16 << 20,
        ).reshape(rows, group, width)

    gated = kernel_call(
        scan_body,
        jax.ShapeDtypeStruct((rows, cols), BF16),
        (step, act, maps, read, decay_rate, entering, skip_gain, gate_in),

        scratch=[
            pltpu.VMEM((rows, cols), F32),
            pltpu.VMEM((rows, count, 128), F32),
            pltpu.VMEM((span * count, cols), BF16),
        ],
        nbytes=16 << 20,
    )
    mamba_out = lax.ppermute(gated, "pipe", [(i, (i + 1) % pipes) for i in range(pipes)])
    far = attend(other_q, 1, gated)
    far_sent = lax.ppermute(
        far,
        ("pipe", "zc"),
        [(2 * i + j, 2 * ((i + 1) % pipes) + 1 - j) for i in range(pipes) for j in range(2)],
    )
    near = attend(own_q, 0, gated)
    near = lax.ppermute(near, "pipe", [(i, (i + 1) % pipes) for i in range(pipes)])
    far = far_sent
    first = jnp.where(zc == 0, near, far)
    second = jnp.where(zc == 0, far, near)
    attended = jnp.concatenate([first, second], axis=1)
    return (attended[None], mamba_out[None])


def solution(mesh):
    pipes, places, parts = mesh.devices.shape
    split = Mesh(
        mesh.devices.reshape(pipes, places // 4, 2, 2, parts), ("pipe", "zh", "zc", "core", "tp")
    )
    return jax.shard_map(
        per_device,
        mesh=split,
        in_specs=(
            P("pipe", CTX, "tp", None),
            P("pipe", None, CTX, "tp", None),
            P("pipe", CTX, "tp"),
            P("pipe", CTX, "tp"),
            P("pipe", CTX, None),
            P("pipe", None, "tp"),
            P("pipe", "tp"),
            P("pipe", None, "tp"),
            P("pipe", None, "tp"),
            P("pipe", "tp"),
            P("pipe", "tp", None),
            P("pipe", "tp"),
        ),
        out_specs=(P("pipe", CTX, "tp", None), P("pipe", CTX, "tp")),
        check_vma=False,
    )
```

```python
import functools
import math

import jax
import jax.numpy as jnp
from jax import lax
from jax.experimental import pallas as pl
from jax.experimental.pallas import tpu as pltpu
from jax.sharding import Mesh, PartitionSpec as P

LOG2E = math.log2(math.e)
CTX = ("zh", "zc", "core")
HALO = 16
F32 = jnp.float32
BF16 = jnp.bfloat16
VMEM = pl.BlockSpec(memory_space=pltpu.VMEM)
SMEM = pl.BlockSpec(memory_space=pltpu.SMEM)


def kernel_call(body, out_shape, args, specs=None, scratch=(), flops=0, nbytes=0, limit=48):
    outs = out_shape if isinstance(out_shape, (tuple, list)) else (out_shape,)
    return pl.pallas_call(
        body,
        out_shape=out_shape,
        in_specs=specs or [VMEM] * len(args),
        out_specs=jax.tree.map(lambda _: VMEM, out_shape),
        scratch_shapes=list(scratch),
        compiler_params=pltpu.CompilerParams(vmem_limit_bytes=limit << 20),
        cost_estimate=pl.CostEstimate(flops=flops, bytes_accessed=nbytes, transcendentals=0),
    )(*args)


def step_body(low_ref, weight_ref, bias_ref, after_ref, step_ref):
    cols = weight_ref.shape[1]
    width = 512
    for at in range(0, cols, width):
        v = jnp.dot(low_ref[...], weight_ref[:, at : at + width], preferred_element_type=F32)
        v = v + bias_ref[:, at : at + width]
        step_ref[:, at : at + width] = jnp.maximum(v, 0.0) + jnp.log1p(jnp.exp(-jnp.abs(v)))


def conv_body(x_ref, halo_ref, weight_ref, bias_ref, proj_ref, act_ref, read_ref):
    rows, cols = x_ref.shape
    taps = weight_ref.shape[0]
    width = 256
    total = jnp.zeros(read_ref.shape[1:], F32)
    for at in range(0, cols, width):
        lanes = slice(at, at + width)
        padded = jnp.concatenate([halo_ref[:, lanes].astype(F32), x_ref[:, lanes].astype(F32)], axis=0)
        v = bias_ref[:, lanes]
        for tap in range(taps):
            first = HALO - (taps - 1) + tap
            v = v + weight_ref[tap : tap + 1, lanes] * padded[first : first + rows]
        act = (v / (1.0 + jnp.exp(-v))).astype(BF16)
        act_ref[:, lanes] = act
        total = total + lax.dot_general(
            proj_ref[:, lanes], act, (((1,), (1,)), ((), ())), preferred_element_type=F32
        )
    for part in range(read_ref.shape[0]):
        read_ref[part] = total


def wide(row, count):
    return jnp.broadcast_to(row, (count, row.shape[1]))


def spread_entry(maps_ref, entry_ref):
    maps = functools.reduce(jnp.add, [maps_ref[part] for part in range(maps_ref.shape[0])])
    rows, count, lanes = entry_ref.shape
    for row in range(rows):
        entry_ref[row] = jnp.broadcast_to(maps[:count, row : row + 1], (count, lanes))
    return maps


def local_body(step_ref, act_ref, maps_ref, rate_ref, out_ref, drive_ref, entry_ref):
    rows, cols = step_ref.shape
    count = rate_ref.shape[0]
    drive_ref[...] = step_ref[...] * act_ref[...].astype(F32)
    spread_entry(maps_ref, entry_ref)
    rate = rate_ref[...] * -LOG2E

    def block(at, carry):
        state, elapsed = carry
        base = pl.multiple_of(at * 16, 16)
        for i in range(16):
            step = wide(step_ref[pl.ds(base + i, 1), :], count)
            drive = wide(drive_ref[pl.ds(base + i, 1), :], count)
            entry = jnp.concatenate([entry_ref[base + i]] * (cols // 128), axis=1)
            state = jnp.exp2(rate * step) * state + entry * drive
            elapsed = elapsed + step
        return state, elapsed

    zero = jnp.zeros((count, cols), F32)
    state, elapsed = lax.fori_loop(0, rows // 16, block, (zero, zero))
    decay = jnp.exp2(rate * elapsed)
    half = count // 2
    for part in range(2 * cols // 128):
        lanes = slice(part // 2 * 128, part // 2 * 128 + 128)
        top = part % 2 * half
        both = jnp.concatenate([state[top : top + half, lanes], decay[top : top + half, lanes]], axis=0)
        out_ref[part] = both.astype(out_ref.dtype)


def prefix_body(in_ref, out_ref):
    places, both, lanes = in_ref.shape
    half = both // 2
    state = jnp.zeros((half, lanes), F32)
    for place in range(places):
        out_ref[place] = state
        pair = in_ref[place].astype(F32)
        state = pair[half:] * state + pair[:half]


def read_body(maps_ref, asked_ref, after_ref, out_ref):
    count = maps_ref.shape[1] // 2
    shape = (count, out_ref.shape[1])
    maps = functools.reduce(jnp.add, [maps_ref[part, count:] for part in range(maps_ref.shape[0])])
    spread = lax.broadcasted_iota(jnp.int32, shape, 0) == lax.broadcasted_iota(jnp.int32, shape, 1) % count
    read = jnp.dot(maps.T.astype(BF16), spread.astype(BF16), preferred_element_type=F32)
    held_at = lax.broadcasted_iota(jnp.int32, read.shape, 1) // count
    own = held_at == lax.broadcasted_iota(jnp.int32, read.shape, 0) % (shape[1] // count)
    out_ref[...] = jnp.where(own, read, 0.0).astype(BF16)


def scan_body(
    step_ref, act_ref, maps_ref, read_ref, rate_ref, enter_ref, skip_ref, gate_ref, after_ref, out_ref,
    drive_ref, entry_ref, held_ref,
):
    rows, cols = step_ref.shape
    count = rate_ref.shape[0]
    span = held_ref.shape[0] // count
    drive_ref[...] = step_ref[...] * act_ref[...].astype(F32)
    rate = rate_ref[...] * -LOG2E
    spread_entry(maps_ref, entry_ref)
    state = jnp.concatenate(
        [
            jnp.concatenate([enter_ref[2 * block], enter_ref[2 * block + 1]], axis=0)
            for block in range(cols // 128)
        ],
        axis=1,
    )

    def chunk(at, state):
        base = pl.multiple_of(at * span, span)
        for i in range(0, span, 2):
            pair = []
            for j in (i, i + 1):
                step = wide(step_ref[pl.ds(base + j, 1), :], count)
                drive = wide(drive_ref[pl.ds(base + j, 1), :], count)
                entry = jnp.concatenate([entry_ref[base + j]] * (cols // 128), axis=1)
                state = jnp.exp2(rate * step) * state + entry * drive
                pair.append(state)
            held_ref[i * count : (i + 2) * count, :] = jnp.concatenate(pair, axis=0).astype(BF16)
        read = read_ref[pl.ds(base, span), :]
        width = 512
        for lane in range(0, cols, width):
            lanes = slice(lane, lane + width)
            scanned = jnp.dot(read, held_ref[:, lanes], preferred_element_type=F32)
            act = act_ref[pl.ds(base, span), lanes].astype(F32)
            gate = gate_ref[pl.ds(base, span), lanes].astype(F32)
            full = scanned + skip_ref[:, lanes] * act
            out_ref[pl.ds(base, span), lanes] = (full * (gate / (1.0 + jnp.exp(-gate)))).astype(out_ref.dtype)
        return state

    lax.fori_loop(0, rows // span, chunk, state)


def attend_body(place_ref, q_ref, kv_ref, after_ref, out_ref, held_ref, top_ref, acc_ref, *, slot, group):
    cores, slots, _, rows, width = kv_ref.shape[1:]
    zh, zc, core = place_ref[0], place_ref[1], place_ref[2]
    keys = cores * slots * rows
    scale = LOG2E / math.sqrt(width)
    tile = 128
    tiles = [slice(first, first + tile) for first in range(0, q_ref.shape[0], tile)]
    query_block = 2 * (zc ^ slot) + core

    def scores_of(at, lines):
        k = kv_ref[at, :, :, 0].reshape(keys, width)
        return lax.dot_general(q_ref[lines, :], k, (((1,), (1,)), ((), ())), preferred_element_type=F32)

    def folded(s):
        return functools.reduce(jnp.maximum, [s[:, lane : lane + width] for lane in range(0, keys, width)])

    for lines in tiles:
        s = scores_of(zh, lines)
        line = lax.broadcasted_iota(jnp.int32, s.shape, 0) + lines.start
        column = lax.broadcasted_iota(jnp.int32, s.shape, 1)
        query_pos = query_block * rows + line // group
        key_block = 2 * (zc ^ (column // rows % slots)) + column // (rows * slots)
        s = jnp.where(key_block * rows + column % rows <= query_pos, s, -jnp.inf)
        held_ref[zh, lines, :] = s
        top_ref[lines, :] = folded(s)

    def score(at, _):
        for lines in tiles:
            s = scores_of(at, lines)
            held_ref[at, lines, :] = s
            top_ref[lines, :] = jnp.maximum(top_ref[lines, :], folded(s))
        return 0

    lax.fori_loop(0, zh, score, 0)
    for lines in tiles:
        top = jnp.max(top_ref[lines, :], axis=1, keepdims=True) * scale
        top_ref[lines, :] = jnp.broadcast_to(top, (tile, width))
    acc_ref[...] = jnp.zeros_like(acc_ref)
    ones = jnp.ones((keys, width), BF16)

    def weigh(at, _):
        v = jnp.concatenate([kv_ref[at, :, :, 1].reshape(keys, width), ones], axis=1)
        for lines in tiles:
            s, top = held_ref[at, lines, :], top_ref[lines, :]
            p = jnp.concatenate(
                [jnp.exp2(s[:, lane : lane + width] * scale - top).astype(BF16) for lane in range(0, keys, width)],
                axis=1,
            )
            acc_ref[lines, :] += jnp.dot(p, v, preferred_element_type=F32)
        return 0

    lax.fori_loop(0, zh + 1, weigh, 0)
    out_ref[...] = (acc_ref[:, :width] / acc_ref[:, width:]).astype(out_ref.dtype)


def per_device(
    queries,
    key_value,
    mamba_in,
    gate_in,
    step_low,
    step_weight,
    step_bias,
    decay_rate,
    conv_weight,
    conv_bias,
    state_weight,
    skip_gain,
):
    queries, key_value, mamba_in, gate_in = queries[0], key_value[0], mamba_in[0], gate_in[0]
    decay_rate, state_weight = decay_rate[0], state_weight[0]
    rows, heads, width = queries.shape
    kv_heads = key_value.shape[2]
    group = heads // kv_heads
    cols = mamba_in.shape[1]
    count = decay_rate.shape[0]
    parts_tp = lax.axis_size("tp")
    pipes = lax.axis_size("pipe")
    places = lax.axis_size(CTX)
    zh, zc, core = (lax.axis_index(a) for a in CTX)
    swap = [(0, 1), (1, 0)]

    own_kv = lax.dynamic_index_in_dim(key_value, zc, 2, False)
    other_kv = lax.ppermute(lax.dynamic_index_in_dim(key_value, 1 - zc, 2, False), "zc", swap)
    halo = lax.ppermute(mamba_in[rows - HALO :], CTX, [(i, i + 1) for i in range(places - 1)])
    own_kv, other_kv, halo = lax.optimization_barrier((own_kv, other_kv, halo))
    kv = lax.all_gather(jnp.stack([own_kv, other_kv]), ("zh", "core"))
    kv = kv.reshape((lax.axis_size("zh"), lax.axis_size("core")) + kv.shape[1:])

    act, partial = kernel_call(
        conv_body,
        (jax.ShapeDtypeStruct((rows, cols), BF16), jax.ShapeDtypeStruct((parts_tp, 2 * count, rows), F32)),
        (mamba_in, halo, conv_weight[0], conv_bias, state_weight.T),
        nbytes=4 << 20,
    )
    step = kernel_call(
        step_body,
        jax.ShapeDtypeStruct((rows, cols), F32),
        (step_low[0], step_weight[0], step_bias, act),
        flops=2 * rows * cols * step_low.shape[2],
        nbytes=4 << 20,
    )
    maps = lax.all_to_all(partial, "tp", 0, 0, tiled=True)
    queries, maps = lax.optimization_barrier((queries, maps))
    grouped = queries.reshape(rows, kv_heads, group, width)
    own_q = lax.dynamic_index_in_dim(grouped, zc, 1, False)
    other_q = lax.ppermute(lax.dynamic_index_in_dim(grouped, 1 - zc, 1, False), "zc", swap)
    place = jnp.stack([zh, zc, core]).astype(jnp.int32)

    span = 32
    parts = kernel_call(
        local_body,
        jax.ShapeDtypeStruct((2 * cols // 128, count, 128), BF16),
        (step, act, maps, decay_rate),
        scratch=[pltpu.VMEM((rows, cols), F32), pltpu.VMEM((rows, count, 128), F32)],
        nbytes=16 << 20,
    )
    parts = lax.all_to_all(parts, CTX, 0, 0, tiled=True)
    asked = kernel_call(
        prefix_body, jax.ShapeDtypeStruct((places, count // 2, 128), F32), (parts,), nbytes=1 << 20
    )
    read = kernel_call(
        read_body,
        jax.ShapeDtypeStruct((rows, span * count), BF16),
        (maps, asked, other_q),
        nbytes=1 << 20,
    )
    entering = lax.all_to_all(asked, CTX, 0, 0, tiled=True)
    def attend(q, slot, after):
        lines = rows * group
        keys = 4 * rows
        return kernel_call(
            functools.partial(attend_body, slot=slot, group=group),
            jax.ShapeDtypeStruct((lines, width), BF16),
            (place, q.reshape(lines, width), kv, after),
            specs=[SMEM, VMEM, VMEM, VMEM],
            scratch=[
                pltpu.VMEM((places // 4, lines, keys), F32),
                pltpu.VMEM((lines, width), F32),
                pltpu.VMEM((lines, 2 * width), F32),
            ],
            flops=4 * lines * width * rows * places,
            nbytes=16 << 20,
        ).reshape(rows, group, width)

    far = attend(other_q, 1, asked)
    far_sent = lax.ppermute(
        far,
        ("pipe", "zc"),
        [(2 * i + j, 2 * ((i + 1) % pipes) + 1 - j) for i in range(pipes) for j in range(2)],
    )
    gated = kernel_call(
        scan_body,
        jax.ShapeDtypeStruct((rows, cols), BF16),
        (step, act, maps, read, decay_rate, entering, skip_gain, gate_in, far),

        scratch=[
            pltpu.VMEM((rows, cols), F32),
            pltpu.VMEM((rows, count, 128), F32),
            pltpu.VMEM((span * count, cols), BF16),
        ],
        nbytes=16 << 20,
    )
    mamba_out = lax.ppermute(gated, "pipe", [(i, (i + 1) % pipes) for i in range(pipes)])
    near = attend(own_q, 0, far_sent)
    near = lax.ppermute(near, "pipe", [(i, (i + 1) % pipes) for i in range(pipes)])
    far = far_sent
    first = jnp.where(zc == 0, near, far)
    second = jnp.where(zc == 0, far, near)
    attended = jnp.concatenate([first, second], axis=1)
    return (attended[None], mamba_out[None])


def solution(mesh):
    pipes, places, parts = mesh.devices.shape
    split = Mesh(
        mesh.devices.reshape(pipes, places // 4, 2, 2, parts), ("pipe", "zh", "zc", "core", "tp")
    )
    return jax.shard_map(
        per_device,
        mesh=split,
        in_specs=(
            P("pipe", CTX, "tp", None),
            P("pipe", None, CTX, "tp", None),
            P("pipe", CTX, "tp"),
            P("pipe", CTX, "tp"),
            P("pipe", CTX, None),
            P("pipe", None, "tp"),
            P("pipe", "tp"),
            P("pipe", None, "tp"),
            P("pipe", None, "tp"),
            P("pipe", "tp"),
            P("pipe", "tp", None),
            P("pipe", "tp"),
        ),
        out_specs=(P("pipe", CTX, "tp", None), P("pipe", CTX, "tp")),
        check_vma=False,
    )
```
